32 devices in a mesh: grp: 2 (over core), fsdp: 8 (over z, y), tp: 2 (over x).
Axes of the slice: x: 2, y: 2, z: 4, core: 2. Of those that a mesh axis runs over, the one named last changes fastest.
Arguments:
- frames: bfloat16 [2, 2048, 8192], P('grp', 'fsdp'), may hold values from -6 to 6
- rewards: bfloat16 [2048], P('fsdp'), may hold values from -5 to 5
- actions: int32 [2, 2048], P('grp', 'fsdp'), may hold values from 0 to 17
- fractions: int32 [2, 2048, 32], P('grp', 'fsdp'), may hold values from 0 to 63
- episode_shard: int32 [2048, 1], P('fsdp'), may hold values from 0 to 7, as said below
- table: float32 [64], replicated, may hold values from 0.02 to 0.98
- norm_gain: float32 [8192], replicated, may hold values from 0.1 to 1.9
- torso_weight: bfloat16 [8192, 4096], P(('grp', 'fsdp'), 'tp'), may hold values from -0.0625 to 0.0625
- embed_weight: bfloat16 [64, 4096], P(None, 'tp'), may hold values from -0.75 to 0.75
- value_weight: bfloat16 [18, 4096], P(None, 'tp'), may hold values from -0.59765625 to 0.59765625
Outputs:
- torso_grad: float32 [8192, 4096], P(('grp', 'fsdp'), 'tp')
- refreshed_weight: bfloat16 [8192, 4096], P(('grp', 'fsdp', 'tp'))
The draws below stay inside these ranges and needn't reach their ends.
Inputs may be any that keep to these rules, and one draw needn't show every extreme that they name: `episode_shard`: of the rows of one index of fsdp, at most 48 belong to one learner shard, and in every such block some learner shard gets exactly 48; every learner shard gets at least one row from every block.
All inputs are finite; a program needn't handle non-finite values.
Results may differ from the reference program's by a relative error of at most 0.0075.
Values may be sent and summed in bfloat16 or wider, within the bound.
A program may use at most 128 MiB of HBM per device.

```python
import jax
import jax.numpy as jnp
from jax import lax

D = 8192
H = 4096
ACTIONS = 18
COSINES = 64
FRACS = 64
SAMPLES = 32
ROWS_DEV = 256
ROWS = 2048
N_FSDP = 8


def draw_episode_shard(key, part):
    mean_rows = ROWS_DEV // N_FSDP
    half_rows = mean_rows // 2
    pair_count = N_FSDP // 2
    shard_ids = jnp.arange(N_FSDP, dtype=jnp.int32)
    inner = jnp.minimum(shard_ids, N_FSDP - 1 - shard_ids)
    spread = half_rows * (pair_count - inner) // pair_count
    profile = jnp.where(shard_ids < pair_count, mean_rows - spread, mean_rows + spread).astype(jnp.int32)

    def one_block(block_id):
        order_key = jax.random.fold_in(key, 7 * block_id + 1)
        shuffle_key = jax.random.fold_in(key, 7 * block_id + 2)
        perm = jax.random.permutation(order_key, N_FSDP)
        counts = profile[perm]
        bounds = jnp.cumsum(counts).astype(jnp.int32)
        places = jnp.arange(ROWS_DEV, dtype=jnp.int32)
        owner = jnp.sum((places[:, None] >= bounds[None, :]).astype(jnp.int32), axis=1).astype(jnp.int32)
        shuffle = jax.random.permutation(shuffle_key, ROWS_DEV)
        return owner[shuffle]
    blocks = jax.vmap(one_block)(jnp.arange(N_FSDP, dtype=jnp.int32))
    return blocks.reshape(ROWS, 1).astype(jnp.int32)


def touch_ends(array, rng, smallest, top_value):
    shape = array.shape
    spot = [jax.random.randint(jax.random.fold_in(rng, axis), (), 0, shape[axis]) for axis in range(len(shape))]
    array = array.at[tuple(spot)].set(smallest)
    longest = shape.index(max(shape))
    spot[longest] = (spot[longest] + 1) % shape[longest]
    return array.at[tuple(spot)].set(top_value)


def level_of(key, extent, shards, smallest, largest):
    factor_of, own = 1.0, jax.random.fold_in(key, 6)
    for position, parts in shards:
        heights = jnp.exp(jax.random.uniform(jax.random.fold_in(own, position), (parts,), jnp.float32, smallest / len(shards), largest / len(shards)))
        factor_of = factor_of * jnp.repeat(heights, extent[position] // parts).reshape([-1 if axis == position else 1 for axis in range(len(extent))])
    return factor_of


def bell_draw(stream_key, dims, width, limit, pieces=(), kind=jnp.bfloat16):
    drawn = jax.random.normal(stream_key, dims, jnp.float32) * width
    if len(pieces) > 0:
        drawn = level_of(stream_key, dims, pieces, -0.22, 0.18) * drawn
    return jnp.clip(drawn, min=-limit, max=limit).astype(kind)


def setup_inputs(seed: int = 0) -> dict:
    keys = jax.random.split(jax.random.key(seed), 11)
    frames = bell_draw(keys[0], (2, ROWS, D), 1.0, 6.0, ((0, 2), (1, 8)))
    rewards = bell_draw(keys[1], (ROWS,), 1.0, 5.0, ((0, 8),))
    actions = touch_ends(jax.random.randint(keys[2], (2, ROWS), 0, ACTIONS), jax.random.fold_in(keys[2], 1), 0, ACTIONS - 1).astype(jnp.int32)
    fractions = touch_ends(jax.random.randint(keys[3], (2, ROWS, SAMPLES), 0, FRACS), jax.random.fold_in(keys[3], 1), 0, FRACS - 1).astype(jnp.int32)
    episode_shard = draw_episode_shard(jax.random.fold_in(keys[10], 71), 0)
    table = jnp.clip(jax.random.uniform(keys[5], (FRACS,), jnp.float32, 0.02, 0.98), 0.02, 0.98)
    norm_gain = jnp.clip(1.0 + 0.18 * jax.random.normal(keys[6], (D,), jnp.float32), 0.1, 1.9)
    torso_weight = bell_draw(keys[7], (D, H), D ** -0.5, 0.0625, ((0, 16), (1, 2)))
    embed_weight = bell_draw(keys[8], (COSINES, H), COSINES ** -0.5, 0.75, ((1, 2),))
    value_weight = bell_draw(keys[9], (ACTIONS, H), 0.1, 0.59765625, ((1, 2),))
    return {"frames": frames, "rewards": rewards, "actions": actions, "fractions": fractions, "episode_shard": episode_shard, "table": table, "norm_gain": norm_gain, "torso_weight": torso_weight, "embed_weight": embed_weight, "value_weight": value_weight}


def forward_part(frames_part, action_part, fraction_part, norm_gain, torso_weight, value_weight, embedding):
    values = frames_part.astype(jnp.float32)
    mean_square = lax.optimization_barrier(jnp.mean(values * values, axis=-1, keepdims=True))
    normed = (values * lax.rsqrt(mean_square + 1e-05) * norm_gain).astype(jnp.bfloat16)
    preact = jnp.dot(normed, torso_weight, preferred_element_type=jnp.float32)
    choose_mask = (action_part[:, None] == jnp.arange(ACTIONS, dtype=jnp.int32)[None, :]).astype(jnp.bfloat16)
    picked = jnp.dot(choose_mask, value_weight, preferred_element_type=jnp.float32)
    weighted = (jax.nn.silu(preact) * picked).astype(jnp.bfloat16)
    table_values = jnp.dot(weighted, embedding.T, preferred_element_type=jnp.float32)
    selector = (fraction_part[:, :, None] == jnp.arange(FRACS, dtype=jnp.int32)[None, None, :]).astype(jnp.float32)
    quant = jnp.einsum('mj,mtj->mt', table_values, selector, precision=lax.Precision.HIGHEST)
    return (normed, preact, picked, selector, quant)

def reference(frames, rewards, actions, fractions, episode_shard, table, norm_gain, torso_weight, embed_weight, value_weight):
    destination = episode_shard[:, 0]
    onehot = (destination[:, None] == jnp.arange(N_FSDP, dtype=jnp.int32)[None, :]).astype(jnp.float32)
    counts = lax.optimization_barrier(jnp.sum(onehot, axis=0))
    row_weight = jnp.dot(onehot, float(ROWS_DEV) / counts, precision=lax.Precision.HIGHEST)
    cosine = jnp.cos(jnp.pi * jnp.arange(COSINES, dtype=jnp.float32)[None, :] * table[:, None]).astype(jnp.bfloat16)
    embedding = jax.nn.relu(jnp.dot(cosine, embed_weight, preferred_element_type=jnp.float32)).astype(jnp.bfloat16)
    target_out = forward_part(frames[0], actions[0], fractions[0], norm_gain, torso_weight, value_weight, embedding)
    normed, preact, picked, selector, online_quant = forward_part(frames[1], actions[1], fractions[1], norm_gain, torso_weight, value_weight, embedding)
    target_quant = target_out[4]
    levels = jnp.einsum('mtj,j->mt', selector, table, precision=lax.Precision.HIGHEST)
    target_value = rewards.astype(jnp.float32)[:, None] + 0.99 * target_quant
    errors = target_value[:, None, :] - online_quant[:, :, None]
    weight = jnp.abs(levels[:, :, None] - (errors < 0).astype(jnp.float32))
    grad_quant = -row_weight[:, None] * lax.optimization_barrier(jnp.sum(weight * jnp.clip(errors, -1.0, 1.0), axis=-1))
    grad_table = jnp.einsum('mi,mij->mj', grad_quant, selector, precision=lax.Precision.HIGHEST)
    grad_feature = jnp.dot(grad_table, embedding.astype(jnp.float32), precision=lax.Precision.HIGHEST)
    gate_value = jax.nn.sigmoid(preact)
    grad_preact = (grad_feature * picked * gate_value * (1.0 + preact * (1.0 - gate_value))).astype(jnp.bfloat16)
    torso_grad = jnp.dot(normed.T, grad_preact, preferred_element_type=jnp.float32)
    refreshed_weight = (torso_weight.astype(jnp.float32) - 0.01 * torso_grad).astype(jnp.bfloat16)
    return (torso_grad, refreshed_weight)
```

```python
import jax
import jax.numpy as jnp
from jax import lax
from jax.sharding import PartitionSpec as P

ACTIONS = 18
COSINES = 64
FRACS = 64
PARTS = (2, 1, 1)


def rotate(value, axis, step):
    size = lax.axis_size(axis)
    return lax.ppermute(value, axis, [(s, (s + step) % size) for s in range(size)])


def swap_half(value, group_index):
    half = value.shape[0] // 2
    kept = lax.dynamic_slice_in_dim(value, group_index * half, half, 0)
    sent = lax.dynamic_slice_in_dim(value, (1 - group_index) * half, half, 0)
    got = rotate(sent, "grp", 1)
    first = group_index == 0
    return jnp.concatenate([jnp.where(first, kept, got), jnp.where(first, got, kept)], axis=0)


def arrange(pieces, index):
    total = len(pieces)
    blocks = []
    for source in range(total):
        offset = lax.rem(index - source + total, total)
        block = pieces[0]
        for step in range(1, total):
            block = jnp.where(offset == step, pieces[step], block)
        blocks.append(block)
    return blocks


def bounds(columns):
    unit = columns // sum(PARTS)
    result, start = [], 0
    for part in PARTS:
        result.append((start, start + part * unit))
        start += part * unit
    return result


def shards(
    frames,
    rewards,
    actions,
    fractions,
    episode_shard,
    table,
    norm_gain,
    torso_weight,
    embed_weight,
    value_weight,
):
    shard_total = lax.axis_size("fsdp")
    tp_total = lax.axis_size("tp")
    group_index = lax.axis_index("grp")
    tp_index = lax.axis_index("tp")
    block, columns = torso_weight.shape
    spans = bounds(columns)
    gathered = [
        lax.all_gather(torso_weight[:, a:b], ("grp", "fsdp"), axis=0, tiled=True) for a, b in spans
    ]

    rows_block = episode_shard.shape[0]
    half = rows_block // 2
    destination = episode_shard[:, 0]
    lanes = jnp.arange(shard_total, dtype=jnp.int32)
    onehot = (destination[:, None] == lanes[None, :]).astype(jnp.float32)
    counts = lax.psum(jnp.sum(onehot, axis=0), "fsdp")
    row_weight = jnp.dot(
        lax.dynamic_slice_in_dim(onehot, group_index * half, half, 0),
        float(rows_block) / counts,
        precision=lax.Precision.HIGHEST,
    )
    reward_rows = lax.dynamic_slice_in_dim(rewards, group_index * half, half, 0)

    action_rows = swap_half(actions[0], group_index)
    fraction_rows = swap_half(fractions[0], group_index)
    values = swap_half(frames[0], group_index).astype(jnp.float32)
    mean_square = jnp.mean(values * values, axis=-1, keepdims=True)
    normed = (values * lax.rsqrt(mean_square + 1e-05) * norm_gain).astype(jnp.bfloat16)

    rows_part = half // tp_total
    own_rows = lax.dynamic_slice_in_dim(normed, half + tp_index * rows_part, rows_part, 0)
    outgoing = own_rows.reshape(rows_part, 2 * shard_total, block).transpose(1, 0, 2)
    incoming = lax.all_to_all(outgoing, ("grp", "fsdp"), split_axis=0, concat_axis=0, tiled=True)
    pieces = [incoming] + [rotate(incoming, "tp", step) for step in range(1, tp_total)]
    columns_all = jnp.concatenate(
        [piece[:, None] for piece in arrange(pieces, tp_index)], axis=1
    ).reshape(2 * shard_total * half, block)

    choose_mask = (action_rows[:, None] == jnp.arange(ACTIONS, dtype=jnp.int32)[None, :]).astype(
        jnp.bfloat16
    )
    picked = jnp.dot(choose_mask, value_weight, preferred_element_type=jnp.float32)
    cosine = jnp.cos(
        jnp.pi * jnp.arange(COSINES, dtype=jnp.float32)[None, :] * table[:, None]
    ).astype(jnp.bfloat16)
    embedding = jax.nn.relu(
        jnp.dot(cosine, embed_weight, preferred_element_type=jnp.float32)
    ).astype(jnp.bfloat16)
    selector = (
        fraction_rows[:, :, None] == jnp.arange(FRACS, dtype=jnp.int32)[None, None, :]
    ).astype(jnp.float32)
    levels = jnp.einsum("mtj,j->mt", selector[half:], table, precision=lax.Precision.HIGHEST)

    gathered[0], columns_all, picked, embedding, levels, row_weight = lax.optimization_barrier(
        (gathered[0], columns_all, picked, embedding, levels, row_weight)
    )
    table_values = None
    preacts = []
    for (a, b), weight_columns in zip(spans, gathered):
        preact = jnp.dot(normed, weight_columns, preferred_element_type=jnp.float32)
        weighted = (jax.nn.silu(preact) * picked[:, a:b]).astype(jnp.bfloat16)
        term = lax.dot_general(
            weighted,
            embedding[:, a:b],
            (((1,), (1,)), ((), ())),
            preferred_element_type=jnp.float32,
        )
        table_values = term if table_values is None else table_values + term
        preacts.append(preact[half:])

    quant = jnp.einsum("mj,mtj->mt", table_values, selector, precision=lax.Precision.HIGHEST)
    others = [rotate(quant, "tp", step) for step in range(1, tp_total)]
    for other in others:
        quant = quant + other
    target_quant, online_quant = quant[:half], quant[half:]
    target_value = reward_rows.astype(jnp.float32)[:, None] + 0.99 * target_quant
    errors = target_value[:, None, :] - online_quant[:, :, None]
    weight = jnp.abs(levels[:, :, None] - (errors < 0).astype(jnp.float32))
    grad_quant = -row_weight[:, None] * jnp.sum(weight * jnp.clip(errors, -1.0, 1.0), axis=-1)
    grad_table = jnp.einsum(
        "mi,mij->mj", grad_quant, selector[half:], precision=lax.Precision.HIGHEST
    )

    rows_all = []
    for (a, b), preact in zip(spans, preacts):
        grad_feature = jnp.dot(
            grad_table, embedding[:, a:b].astype(jnp.float32), precision=lax.Precision.HIGHEST
        )
        gate_value = jax.nn.sigmoid(preact)
        grad_preact = (
            grad_feature * picked[half:, a:b] * gate_value * (1.0 + preact * (1.0 - gate_value))
        ).astype(jnp.bfloat16)
        rows_all.append(lax.all_gather(grad_preact, ("grp", "fsdp"), axis=0, tiled=True))

    grads = []
    refreshed = [[] for _ in range(tp_total)]
    share = block // tp_total
    for (a, b), rows in zip(spans, rows_all):
        grad = lax.dot_general(
            columns_all, rows, (((0,), (0,)), ((), ())), preferred_element_type=jnp.float32
        )
        updated = (torso_weight[:, a:b].astype(jnp.float32) - 0.01 * grad).astype(jnp.bfloat16)
        pieces = []
        for step in range(tp_total):
            target = lax.rem(tp_index + step, tp_total)
            piece = lax.dynamic_slice_in_dim(updated, target * share, share, 0)
            pieces.append(rotate(piece, "tp", step) if step else piece)
        for source, piece in enumerate(arrange(pieces, tp_index)):
            refreshed[source].append(piece)
        grads.append(grad)
    torso_grad = jnp.concatenate(grads, axis=1)
    refreshed_weight = jnp.concatenate([piece for row in refreshed for piece in row], axis=1)
    return (torso_grad, refreshed_weight)


def solution(mesh):
    placed = (
        P("grp", "fsdp", None),
        P("fsdp"),
        P("grp", "fsdp"),
        P("grp", "fsdp", None),
        P("fsdp", None),
        P(),
        P(),
        P(("grp", "fsdp"), "tp"),
        P(None, "tp"),
        P(None, "tp"),
    )
    return jax.shard_map(
        shards,
        mesh=mesh,
        in_specs=placed,
        out_specs=(P(("grp", "fsdp"), "tp"), P(("grp", "fsdp", "tp"), None)),
        check_vma=False,
    )
```

```python
import jax
import jax.numpy as jnp
from jax import lax
from jax.sharding import PartitionSpec as P

ACTIONS = 18
COSINES = 64
FRACS = 64
PARTS = (1,)


def rotate(value, axis, step):
    size = lax.axis_size(axis)
    return lax.ppermute(value, axis, [(s, (s + step) % size) for s in range(size)])


def swap_half(value, group_index):
    half = value.shape[0] // 2
    kept = lax.dynamic_slice_in_dim(value, group_index * half, half, 0)
    sent = lax.dynamic_slice_in_dim(value, (1 - group_index) * half, half, 0)
    got = rotate(sent, "grp", 1)
    first = group_index == 0
    return jnp.concatenate([jnp.where(first, kept, got), jnp.where(first, got, kept)], axis=0)


def arrange(pieces, index):
    total = len(pieces)
    blocks = []
    for source in range(total):
        offset = lax.rem(index - source + total, total)
        block = pieces[0]
        for step in range(1, total):
            block = jnp.where(offset == step, pieces[step], block)
        blocks.append(block)
    return blocks


def bounds(columns):
    unit = columns // sum(PARTS)
    result, start = [], 0
    for part in PARTS:
        result.append((start, start + part * unit))
        start += part * unit
    return result


def shards(
    frames,
    rewards,
    actions,
    fractions,
    episode_shard,
    table,
    norm_gain,
    torso_weight,
    embed_weight,
    value_weight,
):
    shard_total = lax.axis_size("fsdp")
    tp_total = lax.axis_size("tp")
    group_index = lax.axis_index("grp")
    tp_index = lax.axis_index("tp")
    block, columns = torso_weight.shape
    spans = bounds(columns)
    gathered = [
        lax.all_gather(torso_weight[:, a:b], ("grp", "fsdp"), axis=0, tiled=True) for a, b in spans
    ]

    rows_block = episode_shard.shape[0]
    half = rows_block // 2
    destination = episode_shard[:, 0]
    lanes = jnp.arange(shard_total, dtype=jnp.int32)
    onehot = (destination[:, None] == lanes[None, :]).astype(jnp.float32)
    counts = lax.psum(jnp.sum(onehot, axis=0), "fsdp")
    row_weight = jnp.dot(
        lax.dynamic_slice_in_dim(onehot, group_index * half, half, 0),
        float(rows_block) / counts,
        precision=lax.Precision.HIGHEST,
    )
    reward_rows = lax.dynamic_slice_in_dim(rewards, group_index * half, half, 0)

    action_rows = swap_half(actions[0], group_index)
    fraction_rows = swap_half(fractions[0], group_index)
    values = swap_half(frames[0], group_index).astype(jnp.float32)
    mean_square = jnp.mean(values * values, axis=-1, keepdims=True)
    normed = (values * lax.rsqrt(mean_square + 1e-05) * norm_gain).astype(jnp.bfloat16)

    rows_part = half // tp_total
    own_rows = lax.dynamic_slice_in_dim(normed, half + tp_index * rows_part, rows_part, 0)
    outgoing = own_rows.reshape(rows_part, 2 * shard_total, block).transpose(1, 0, 2)
    incoming = lax.all_to_all(outgoing, ("grp", "fsdp"), split_axis=0, concat_axis=0, tiled=True)
    pieces = [incoming] + [rotate(incoming, "tp", step) for step in range(1, tp_total)]
    columns_all = jnp.concatenate(
        [piece[:, None] for piece in arrange(pieces, tp_index)], axis=1
    ).reshape(2 * shard_total * half, block)

    choose_mask = (action_rows[:, None] == jnp.arange(ACTIONS, dtype=jnp.int32)[None, :]).astype(
        jnp.bfloat16
    )
    picked = jnp.dot(choose_mask, value_weight, preferred_element_type=jnp.float32)
    cosine = jnp.cos(
        jnp.pi * jnp.arange(COSINES, dtype=jnp.float32)[None, :] * table[:, None]
    ).astype(jnp.bfloat16)
    embedding = jax.nn.relu(
        jnp.dot(cosine, embed_weight, preferred_element_type=jnp.float32)
    ).astype(jnp.bfloat16)
    selector = (
        fraction_rows[:, :, None] == jnp.arange(FRACS, dtype=jnp.int32)[None, None, :]
    ).astype(jnp.float32)
    levels = jnp.einsum("mtj,j->mt", selector[half:], table, precision=lax.Precision.HIGHEST)

    gathered[0], columns_all, picked, embedding, levels, row_weight = lax.optimization_barrier(
        (gathered[0], columns_all, picked, embedding, levels, row_weight)
    )
    table_values = None
    preacts = []
    for (a, b), weight_columns in zip(spans, gathered):
        preact = jnp.dot(normed, weight_columns, preferred_element_type=jnp.float32)
        weighted = (jax.nn.silu(preact) * picked[:, a:b]).astype(jnp.bfloat16)
        term = lax.dot_general(
            weighted,
            embedding[:, a:b],
            (((1,), (1,)), ((), ())),
            preferred_element_type=jnp.float32,
        )
        table_values = term if table_values is None else table_values + term
        preacts.append(preact[half:])

    quant = jnp.einsum("mj,mtj->mt", table_values, selector, precision=lax.Precision.HIGHEST)
    others = [rotate(quant, "tp", step) for step in range(1, tp_total)]
    for other in others:
        quant = quant + other
    target_quant, online_quant = quant[:half], quant[half:]
    target_value = reward_rows.astype(jnp.float32)[:, None] + 0.99 * target_quant
    errors = target_value[:, None, :] - online_quant[:, :, None]
    weight = jnp.abs(levels[:, :, None] - (errors < 0).astype(jnp.float32))
    grad_quant = -row_weight[:, None] * jnp.sum(weight * jnp.clip(errors, -1.0, 1.0), axis=-1)
    grad_table = jnp.einsum(
        "mi,mij->mj", grad_quant, selector[half:], precision=lax.Precision.HIGHEST
    )

    rows_all = []
    for (a, b), preact in zip(spans, preacts):
        grad_feature = jnp.dot(
            grad_table, embedding[:, a:b].astype(jnp.float32), precision=lax.Precision.HIGHEST
        )
        gate_value = jax.nn.sigmoid(preact)
        grad_preact = (
            grad_feature * picked[half:, a:b] * gate_value * (1.0 + preact * (1.0 - gate_value))
        ).astype(jnp.bfloat16)
        rows_all.append(lax.all_gather(grad_preact, ("grp", "fsdp"), axis=0, tiled=True))

    grads = []
    refreshed = [[] for _ in range(tp_total)]
    share = block // tp_total
    for (a, b), rows in zip(spans, rows_all):
        grad = lax.dot_general(
            columns_all, rows, (((0,), (0,)), ((), ())), preferred_element_type=jnp.float32
        )
        updated = (torso_weight[:, a:b].astype(jnp.float32) - 0.01 * grad).astype(jnp.bfloat16)
        pieces = []
        for step in range(tp_total):
            target = lax.rem(tp_index + step, tp_total)
            piece = lax.dynamic_slice_in_dim(updated, target * share, share, 0)
            pieces.append(rotate(piece, "tp", step) if step else piece)
        for source, piece in enumerate(arrange(pieces, tp_index)):
            refreshed[source].append(piece)
        grads.append(grad)
    torso_grad = jnp.concatenate(grads, axis=1)
    refreshed_weight = jnp.concatenate([piece for row in refreshed for piece in row], axis=1)
    return (torso_grad, refreshed_weight)


def solution(mesh):
    placed = (
        P("grp", "fsdp", None),
        P("fsdp"),
        P("grp", "fsdp"),
        P("grp", "fsdp", None),
        P("fsdp", None),
        P(),
        P(),
        P(("grp", "fsdp"), "tp"),
        P(None, "tp"),
        P(None, "tp"),
    )
    return jax.shard_map(
        shards,
        mesh=mesh,
        in_specs=placed,
        out_specs=(P(("grp", "fsdp"), "tp"), P(("grp", "fsdp", "tp"), None)),
        check_vma=False,
    )
```

```python
import jax
import jax.numpy as jnp
from jax import lax
from jax.sharding import PartitionSpec as P

ACTIONS = 18
COSINES = 64
FRACS = 64
PARTS = (1,)


def rotate(value, axis, step):
    size = lax.axis_size(axis)
    return lax.ppermute(value, axis, [(s, (s + step) % size) for s in range(size)])


def swap_half(value, group_index):
    half = value.shape[0] // 2
    kept = lax.dynamic_slice_in_dim(value, group_index * half, half, 0)
    sent = lax.dynamic_slice_in_dim(value, (1 - group_index) * half, half, 0)
    got = rotate(sent, "grp", 1)
    first = group_index == 0
    return jnp.concatenate([jnp.where(first, kept, got), jnp.where(first, got, kept)], axis=0)


def ring_order(total):
    return list(range(0, total, 2)) + list(range(total - 1, 0, -2))


def ring_gather(value, total):
    cycle = ring_order(total)
    ahead = [(cycle[i], cycle[(i + 1) % total]) for i in range(total)]
    back = [(b, a) for a, b in ahead]
    pieces, forward, backward = [value], value, value
    for step in range(1, total // 2 + 1):
        forward = lax.ppermute(forward, "fsdp", ahead)
        pieces.append(forward)
        if 2 * step < total:
            backward = lax.ppermute(backward, "fsdp", back)
            pieces.append(backward)
    return pieces


def ring_sources(total, index):
    cycle = ring_order(total)
    table = [None] * total
    for place, owner in enumerate(cycle):
        sources = [owner]
        for step in range(1, total // 2 + 1):
            sources.append(cycle[(place - step) % total])
            if 2 * step < total:
                sources.append(cycle[(place + step) % total])
        table[owner] = sources
    return jnp.asarray(table, dtype=jnp.int32)[index]


def arrange(pieces, index):
    total = len(pieces)
    blocks = []
    for source in range(total):
        offset = lax.rem(index - source + total, total)
        block = pieces[0]
        for step in range(1, total):
            block = jnp.where(offset == step, pieces[step], block)
        blocks.append(block)
    return blocks


def bounds(columns):
    unit = columns // sum(PARTS)
    result, start = [], 0
    for part in PARTS:
        result.append((start, start + part * unit))
        start += part * unit
    return result


def shards(
    frames,
    rewards,
    actions,
    fractions,
    episode_shard,
    table,
    norm_gain,
    torso_weight,
    embed_weight,
    value_weight,
):
    shard_total = lax.axis_size("fsdp")
    tp_total = lax.axis_size("tp")
    group_index = lax.axis_index("grp")
    tp_index = lax.axis_index("tp")
    block, columns = torso_weight.shape
    spans = bounds(columns)
    gathered = [
        lax.all_gather(torso_weight[:, a:b], ("grp", "fsdp"), axis=0, tiled=True) for a, b in spans
    ]

    rows_block = episode_shard.shape[0]
    half = rows_block // 2
    destination = episode_shard[:, 0]
    lanes = jnp.arange(shard_total, dtype=jnp.int32)
    onehot = (destination[:, None] == lanes[None, :]).astype(jnp.float32)
    counts = lax.psum(jnp.sum(onehot, axis=0), "fsdp")
    row_weight = jnp.dot(
        lax.dynamic_slice_in_dim(onehot, group_index * half, half, 0),
        float(rows_block) / counts,
        precision=lax.Precision.HIGHEST,
    )
    reward_rows = lax.dynamic_slice_in_dim(rewards, group_index * half, half, 0)

    action_rows = swap_half(actions[0], group_index)
    fraction_rows = swap_half(fractions[0], group_index)
    values = swap_half(frames[0], group_index).astype(jnp.float32)
    mean_square = jnp.mean(values * values, axis=-1, keepdims=True)
    normed = (values * lax.rsqrt(mean_square + 1e-05) * norm_gain).astype(jnp.bfloat16)

    rows_part = half // tp_total
    own_rows = lax.dynamic_slice_in_dim(normed, half + tp_index * rows_part, rows_part, 0)
    outgoing = own_rows.reshape(rows_part, 2 * shard_total, block).transpose(1, 0, 2)
    incoming = lax.all_to_all(outgoing, ("grp", "fsdp"), split_axis=0, concat_axis=0, tiled=True)
    pieces = [incoming] + [rotate(incoming, "tp", step) for step in range(1, tp_total)]
    columns_all = jnp.concatenate(
        [piece[:, None] for piece in arrange(pieces, tp_index)], axis=1
    ).reshape(2, shard_total, half, block)
    columns_all = jnp.take(columns_all, ring_sources(shard_total, lax.axis_index("fsdp")), axis=1)
    columns_all = columns_all.reshape(2, shard_total * half, block)
    columns_all = jnp.where(group_index == 0, columns_all, columns_all[::-1]).reshape(
        2 * shard_total * half, block
    )

    choose_mask = (action_rows[:, None] == jnp.arange(ACTIONS, dtype=jnp.int32)[None, :]).astype(
        jnp.bfloat16
    )
    picked = jnp.dot(choose_mask, value_weight, preferred_element_type=jnp.float32)
    cosine = jnp.cos(
        jnp.pi * jnp.arange(COSINES, dtype=jnp.float32)[None, :] * table[:, None]
    ).astype(jnp.bfloat16)
    embedding = jax.nn.relu(
        jnp.dot(cosine, embed_weight, preferred_element_type=jnp.float32)
    ).astype(jnp.bfloat16)
    selector = (
        fraction_rows[:, :, None] == jnp.arange(FRACS, dtype=jnp.int32)[None, None, :]
    ).astype(jnp.float32)
    levels = jnp.einsum("mtj,j->mt", selector[half:], table, precision=lax.Precision.HIGHEST)

    gathered[0], columns_all, picked, embedding, levels, row_weight = lax.optimization_barrier(
        (gathered[0], columns_all, picked, embedding, levels, row_weight)
    )
    table_values = None
    preacts = []
    for (a, b), weight_columns in zip(spans, gathered):
        preact = jnp.dot(normed, weight_columns, preferred_element_type=jnp.float32)
        weighted = (jax.nn.silu(preact) * picked[:, a:b]).astype(jnp.bfloat16)
        term = lax.dot_general(
            weighted,
            embedding[:, a:b],
            (((1,), (1,)), ((), ())),
            preferred_element_type=jnp.float32,
        )
        table_values = term if table_values is None else table_values + term
        preacts.append(preact[half:])

    quant = jnp.einsum("mj,mtj->mt", table_values, selector, precision=lax.Precision.HIGHEST)
    others = [rotate(quant, "tp", step) for step in range(1, tp_total)]
    for other in others:
        quant = quant + other
    target_quant, online_quant = quant[:half], quant[half:]
    target_value = reward_rows.astype(jnp.float32)[:, None] + 0.99 * target_quant
    errors = target_value[:, None, :] - online_quant[:, :, None]
    weight = jnp.abs(levels[:, :, None] - (errors < 0).astype(jnp.float32))
    grad_quant = -row_weight[:, None] * jnp.sum(weight * jnp.clip(errors, -1.0, 1.0), axis=-1)
    grad_table = jnp.einsum(
        "mi,mij->mj", grad_quant, selector[half:], precision=lax.Precision.HIGHEST
    )

    rows_all = []
    for (a, b), preact in zip(spans, preacts):
        grad_feature = jnp.dot(
            grad_table, embedding[:, a:b].astype(jnp.float32), precision=lax.Precision.HIGHEST
        )
        gate_value = jax.nn.sigmoid(preact)
        grad_preact = (
            grad_feature * picked[half:, a:b] * gate_value * (1.0 + preact * (1.0 - gate_value))
        ).astype(jnp.bfloat16)
        own = ring_gather(grad_preact, shard_total)
        partner = [rotate(piece, "grp", 1) for piece in own]
        rows_all.append(jnp.concatenate(own + partner, axis=0))

    grads = []
    refreshed = [[] for _ in range(tp_total)]
    share = block // tp_total
    for (a, b), rows in zip(spans, rows_all):
        grad = lax.dot_general(
            columns_all, rows, (((0,), (0,)), ((), ())), preferred_element_type=jnp.float32
        )
        updated = (torso_weight[:, a:b].astype(jnp.float32) - 0.01 * grad).astype(jnp.bfloat16)
        pieces = []
        for step in range(tp_total):
            target = lax.rem(tp_index + step, tp_total)
            piece = lax.dynamic_slice_in_dim(updated, target * share, share, 0)
            pieces.append(rotate(piece, "tp", step) if step else piece)
        for source, piece in enumerate(arrange(pieces, tp_index)):
            refreshed[source].append(piece)
        grads.append(grad)
    torso_grad = jnp.concatenate(grads, axis=1)
    refreshed_weight = jnp.concatenate([piece for row in refreshed for piece in row], axis=1)
    return (torso_grad, refreshed_weight)


def solution(mesh):
    placed = (
        P("grp", "fsdp", None),
        P("fsdp"),
        P("grp", "fsdp"),
        P("grp", "fsdp", None),
        P("fsdp", None),
        P(),
        P(),
        P(("grp", "fsdp"), "tp"),
        P(None, "tp"),
        P(None, "tp"),
    )
    return jax.shard_map(
        shards,
        mesh=mesh,
        in_specs=placed,
        out_specs=(P(("grp", "fsdp"), "tp"), P(("grp", "fsdp", "tp"), None)),
        check_vma=False,
    )
```
